32 devices in a mesh: section: 4 (over z), dp: 8 (over y, x, core).
Axes of the slice: x: 2, y: 2, z: 4, core: 2. Of those that a mesh axis runs over, the one named last changes fastest.
Arguments:
- saved: bfloat16 [4, 32, 4, 8, 384], P('section', 'dp'), may hold values from -6 to 6
- kernels: bfloat16 [4, 384, 3, 3, 384], P('section'), may hold values from -0.109375 to 0.109375
- head: bfloat16 [384, 512], replicated, may hold values from -0.3125 to 0.3125
- counts: int32 [8], P('dp'), may hold values from 1 to 4, as said below
- pairs: int32 [32], P('dp'), may hold values from 0 to 31, as said below
- valid: int32 [32], P('dp'), may hold values 0 or 1
Outputs:
- input_grads: bfloat16 [4, 32, 4, 8, 384], P('section', 'dp')
- weight_grads: float32 [4, 384, 3, 3, 384], P('section', 'dp')
- head_grad: float32 [384, 512], P('dp', 'section')
The draws below stay inside these ranges and needn't reach their ends.
Inputs may be any that keep to these rules, and one draw needn't show every extreme that they name: Slot d * 4 + r holds a record exactly when r < counts[d]; at least one index of dp holds 4 records. pairs[pairs[i]] = i and pairs[i] != i.
All inputs are finite; a program needn't handle non-finite values. No bound on the sum of `valid` on one device may be relied on, other than what follows from the above.
Results may differ from the reference program's by a relative error of at most 0.012.
Values may be sent and summed in bfloat16 or wider, within the bound.
A program may use at most 64 MiB of HBM per device.

```python
import jax
import jax.numpy as jnp
from jax import lax

CH = 384
EMB = 512
KS = 3
PH = 4
PW = 8
CAP = 4
RECS = 32
N_SECTION = 4


def draw_counts(key, part):
    groups = RECS // CAP
    lowest = max(1, CAP // 4)
    first_key, second_key = jax.random.split(key)
    values = jax.random.randint(first_key, (groups,), lowest, CAP + 1)
    fullest = jax.random.randint(second_key, (), 0, groups)
    return jnp.where(jnp.arange(groups) == fullest, CAP, values).astype(jnp.int32)


def draw_pairs(key, part):
    order = jax.random.permutation(key, RECS).astype(jnp.int32)
    mates = order.reshape(RECS // 2, 2)[:, ::-1].reshape(RECS)
    return jnp.zeros((RECS,), jnp.int32).at[order].set(mates)


def place_ends(values, stream_key, smallest, top_value):
    dims = values.shape
    index_at = [jax.random.randint(jax.random.fold_in(stream_key, axis), (), 0, dims[axis]) for axis in range(len(dims))]
    values = values.at[tuple(index_at)].set(smallest)
    longest = dims.index(max(dims))
    index_at[longest] = (index_at[longest] + 1) % dims[longest]
    return values.at[tuple(index_at)].set(top_value)


def level_of(rng, shape, cuts, low, high):
    def one(dim, parts):
        steps = jax.random.uniform(jax.random.fold_in(jax.random.fold_in(rng, 6), dim), (parts,), jnp.float32, low / len(cuts), high / len(cuts))
        return jnp.repeat(jnp.exp(steps), shape[dim] // parts).reshape((-1,) + (1,) * (len(shape) - dim - 1))

    gain = one(*cuts[0])
    for cut in cuts[1:]:
        gain = gain * one(*cut)
    return gain


def scatter_about(rng, extent, deviation, reach, shards=(), kind=jnp.bfloat16):
    result = deviation * jax.random.normal(rng, extent, jnp.float32)
    if shards:
        result = result * level_of(rng, extent, shards, -0.22, 0.18)
    return jnp.clip(result, -reach, reach).astype(kind)


def setup_inputs(seed: int = 0) -> dict:
    arg_keys = jax.random.split(jax.random.key(seed), 7)
    saved = scatter_about(arg_keys[0], (N_SECTION, RECS, PH, PW, CH), 1.0, 6.0, ((0, 4), (1, 8)))
    kernels = scatter_about(arg_keys[1], (N_SECTION, CH, KS, KS, CH), (KS * KS * CH) ** -0.5, 0.109375, ((0, 4),))
    head = scatter_about(arg_keys[2], (CH, EMB), CH ** -0.5, 0.3125)
    counts = draw_counts(jax.random.fold_in(arg_keys[6], 71), 0)
    pairs = draw_pairs(jax.random.fold_in(arg_keys[6], 71), 0)
    valid = place_ends((jax.random.randint(arg_keys[5], (RECS,), 0, 8) < 7).astype(jnp.int32), jax.random.fold_in(arg_keys[5], 1), 0, 1)
    return dict(saved=saved, kernels=kernels, head=head, counts=counts, pairs=pairs, valid=valid)


tau_value = 0.2
loss_scale = 32.0
norm_eps = 1e-06

def conv_apply(inputs, kernel):
    return lax.conv_general_dilated(inputs, kernel, (1, 1), 'SAME', dimension_numbers=('NHWC', 'IHWO', 'NHWC'), preferred_element_type=jnp.float32)

def conv_back(grads, kernel):
    return lax.conv_general_dilated(grads, jnp.flip(kernel, (1, 2)), (1, 1), 'SAME', dimension_numbers=('NHWC', 'OHWI', 'NHWC'), preferred_element_type=jnp.float32)

def kernel_grad(inputs, grads):
    return lax.conv_general_dilated(inputs, grads, (1, 1), ((1, 1), (1, 1)), dimension_numbers=('CHWN', 'IHWO', 'NHWC'), preferred_element_type=jnp.float32)

def reference(saved, kernels, head, counts, pairs, valid):
    slot = jnp.arange(RECS, dtype=jnp.int32)
    owner = slot // CAP
    live = jnp.where((slot - owner * CAP < counts[owner]) & (valid == 1), 1.0, 0.0).astype(jnp.float32)
    slopes = []
    pooled = None
    for layer in range(N_SECTION):
        pre = conv_apply(saved[layer], kernels[layer])
        sigma = jax.nn.sigmoid(pre)
        slopes.append(sigma * (1.0 + pre * (1.0 - sigma)))
        if layer == N_SECTION - 1:
            pooled = lax.optimization_barrier(jnp.mean(saved[layer].astype(jnp.float32) + pre * sigma, axis=(1, 2))).astype(jnp.bfloat16)
    proj = jnp.dot(pooled, head, preferred_element_type=jnp.float32)
    inv = lax.rsqrt(lax.optimization_barrier(jnp.sum(proj * proj, axis=1, keepdims=True)) + norm_eps)
    unit = proj * inv
    unit_b = unit.astype(jnp.bfloat16)
    scores = lax.dot_general(unit_b, unit_b, (((1,), (1,)), ((), ())), preferred_element_type=jnp.float32) / tau_value
    expo = jnp.where(slot[:, None] != slot[None, :], jnp.exp(scores), 0.0)
    total = lax.optimization_barrier(jnp.sum(expo * live[None, :], axis=1))
    share = live * live[pairs]
    coef = lax.optimization_barrier((share / total).astype(jnp.bfloat16)).astype(jnp.float32)
    mixing = expo * (coef[:, None] * live[None, :] + coef[None, :] * live[:, None]) - 2.0 * jnp.where(pairs[:, None] == slot[None, :], share[:, None], 0.0)
    dunit = jnp.dot(mixing.astype(jnp.bfloat16), unit_b, preferred_element_type=jnp.float32) * (loss_scale / tau_value)
    along = lax.optimization_barrier(jnp.sum(unit * dunit, axis=1, keepdims=True))
    dproj = ((dunit - unit * along) * inv).astype(jnp.bfloat16)
    head_grad = lax.dot_general(pooled, dproj, (((0,), (0,)), ((), ())), preferred_element_type=jnp.float32)
    dpooled = lax.dot_general(dproj, head, (((1,), (1,)), ((), ())), preferred_element_type=jnp.float32).astype(jnp.bfloat16)
    top = (dpooled.astype(jnp.float32) / (PH * PW)).astype(jnp.bfloat16)
    cotan = jnp.broadcast_to(top[:, None, None, :], (RECS, PH, PW, CH))
    grads_in = []
    grads_w = []
    for layer in range(N_SECTION - 1, -1, -1):
        dpre = (cotan.astype(jnp.float32) * slopes[layer]).astype(jnp.bfloat16)
        cotan = (cotan.astype(jnp.float32) + conv_back(dpre, kernels[layer])).astype(jnp.bfloat16)
        grads_in.insert(0, cotan)
        grads_w.insert(0, kernel_grad(saved[layer], dpre))
    return (jnp.stack(grads_in), jnp.stack(grads_w), head_grad)
```

```python
import functools

import jax
import jax.numpy as jnp
from jax import lax
from jax.experimental import pallas as pl
from jax.experimental.pallas import tpu as pltpu
from jax.sharding import PartitionSpec as P

TAU = 0.2
LOSS_SCALE = 32.0
EPS = 1e-06
MESH = pl.DeviceIdType.MESH
F32 = jnp.float32
BF16 = jnp.bfloat16


def dot(a, b, ca, cb):
    return lax.dot_general(a, b, (((ca,), (cb,)), ((), ())), preferred_element_type=F32)


def fill_patches(dst_ref, v, dims, flip):
    recs, ph, pw = dims
    rows, ch = v.shape
    w = lax.broadcasted_iota(jnp.int32, (rows, ch), 0) % pw
    for j in range(3):
        if j == 1:
            vj = v
        elif j == 0:
            vj = jnp.where(w > 0, pltpu.roll(v, 1, 0), 0.0)
        else:
            vj = jnp.where(w < pw - 1, pltpu.roll(v, rows - 1, 0), 0.0)
        cells = vj.reshape(recs, ph, pw, ch)
        edge = jnp.zeros((recs, 1, pw, ch), F32)
        for i in range(3):
            if i == 1:
                vij = cells
            elif i == 0:
                vij = jnp.concatenate([edge, cells[:, : ph - 1]], axis=1)
            else:
                vij = jnp.concatenate([cells[:, 1:], edge], axis=1)
            tap = 3 * i + j
            if flip:
                tap = 8 - tap
            dst_ref[:, tap * ch : (tap + 1) * ch] = vij.reshape(rows, ch).astype(BF16)


def body(cfg, x_ref, k_hbm, head_ref, counts_ref, pairs_ref, valid_ref,
         dx_ref, wg_ref, hg_ref,
         k_ref, kt_ref, patch_ref, slope_ref, pooled_ref, g_ref, dproj_ref, pt_ref,
         hgs_ref, hgr_ref, xt_ref, xg_ref, lhs_ref, dg_ref, acc_ref, cot_ref, relay_ref, out_ref,
         k_sem, gs_sem, gr_sem, hs_sem, hr_sem, xs_sem, xr_sem, ds_sem, dr_sem, cs_sem, cr_sem):
    S, D, cap, ph, pw, ch, emb, cw, cp = cfg
    rows = cap * ph * pw
    sec = lax.axis_index("section")
    rank = lax.axis_index("dp")
    last = S - 1

    def peer(off):
        return lax.rem(rank + off, D)

    def source(off):
        return lax.rem(rank + D - off, D)

    k_copies = []
    for i in range(3):
        cpy = pltpu.make_async_copy(k_hbm.at[3 * i : 3 * i + 3], k_ref.at[3 * i : 3 * i + 3], k_sem.at[i])
        cpy.start()
        k_copies.append(cpy)

    barrier = pltpu.get_barrier_semaphore()
    for off in range(1, D):
        pl.semaphore_signal(barrier, inc=1, device_id=(sec, peer(off)), device_id_type=MESH)
    for off in range(1, S):
        pl.semaphore_signal(barrier, inc=1, device_id=(lax.rem(sec + off, S), rank), device_id_type=MESH)

    x = x_ref[0].astype(F32).reshape(rows, ch)
    fill_patches(patch_ref, x, (cap, ph, pw), False)
    pre = None
    for i in range(3):
        k_copies[i].wait()
        kk = k_ref[3 * i : 3 * i + 3].reshape(3 * ch, ch)
        term = dot(patch_ref[:, 3 * i * ch : 3 * (i + 1) * ch], kk, 1, 0)
        pre = term if pre is None else pre + term
    sig = 1.0 / (1.0 + jnp.exp(-pre))
    slope_ref[...] = sig * (1.0 + pre * (1.0 - sig))

    pl.semaphore_wait(barrier, D - 1 + S - 1)

    def pooled_copy(off):
        return pltpu.make_async_remote_copy(
            src_ref=g_ref.at[rank], dst_ref=g_ref.at[rank],
            send_sem=gs_sem.at[off - 1], recv_sem=gr_sem.at[off - 1],
            device_id=(sec, peer(off)), device_id_type=MESH)

    @pl.when(sec == last)
    def _():
        y = x + pre * sig
        mean = jnp.sum(y.reshape(cap, ph * pw, ch), axis=1) * (1.0 / (ph * pw))
        mean = mean.astype(BF16).astype(F32)
        pooled_ref[...] = jnp.zeros(pooled_ref.shape, F32)
        pooled_ref[0:cap, :ch] = mean
        row = lax.broadcasted_iota(jnp.int32, (8, 128), 0)
        lane = lax.broadcasted_iota(jnp.int32, (8, 128), 1)
        meta = jnp.where(lane == 1, -1.0, 0.0)
        for r in range(cap):
            live = jnp.where((r < counts_ref[0]) & (valid_ref[r] == 1), 1.0, 0.0)
            p = pairs_ref[r]
            pid = ((p // cap) * 8 + p % cap).astype(F32)
            meta = jnp.where((row == r) & (lane == 0), live, meta)
            meta = jnp.where((row == r) & (lane == 1), pid, meta)
        pooled_ref[:, ch:] = meta
        g_ref[rank] = pooled_ref[...]
        for off in range(1, D):
            pooled_copy(off).start()

    def x_copy(off):
        return pltpu.make_async_remote_copy(
            src_ref=xt_ref.at[peer(off)], dst_ref=xg_ref.at[rank],
            send_sem=xs_sem.at[off - 1], recv_sem=xr_sem.at[off - 1],
            device_id=(sec, peer(off)), device_id_type=MESH)

    xt = x.T
    for p in range(D):
        blk = xt[p * cw : (p + 1) * cw]
        if cp != cw:
            blk = jnp.concatenate([blk, jnp.zeros((cp - cw, rows), F32)], axis=0)
        xt_ref[p] = blk.astype(BF16)
    xg_ref[rank] = xt_ref[rank]
    for off in range(1, D):
        x_copy(off).start()

    for t in range(9):
        kt_ref[t * ch : (t + 1) * ch, :] = k_ref[t].T

    ew = emb // S

    def head_copy(off):
        to = lax.rem(sec + off, S)
        return pltpu.make_async_remote_copy(
            src_ref=hgs_ref.at[to], dst_ref=hgr_ref,
            send_sem=hs_sem.at[off - 1], recv_sem=hr_sem.at[0],
            device_id=(to, rank), device_id_type=MESH)

    @pl.when(sec == last)
    def _():
        for off in range(1, D):
            pooled_copy(off).wait()
        n = D * 8
        g = g_ref[...].reshape(n, ch + 128)
        pooled = g[:, :ch].astype(BF16)
        meta = g[:, ch:]
        meta_t = meta.T
        live_col, pair_col = meta[:, 0:1], meta[:, 1:2]
        live_row, pair_row = meta_t[0:1, :], meta_t[1:2, :]
        ii = lax.broadcasted_iota(jnp.int32, (n, n), 0)
        jj = lax.broadcasted_iota(jnp.int32, (n, n), 1)
        head = head_ref[...]
        proj = dot(pooled, head, 1, 0)
        inv = lax.rsqrt(jnp.sum(proj * proj, axis=1, keepdims=True) + EPS)
        unit = proj * inv
        unit_b = unit.astype(BF16)
        scores = dot(unit_b, unit_b, 1, 1) / TAU
        expo = jnp.where(ii != jj, jnp.exp(scores), 0.0)
        is_mate = pair_col == jj.astype(F32)
        is_mate_t = pair_row == ii.astype(F32)
        total_col = jnp.sum(expo * live_row, axis=1, keepdims=True)
        total_row = jnp.sum(expo * live_col, axis=0, keepdims=True)
        share_col = live_col * jnp.sum(jnp.where(is_mate, live_row, 0.0), axis=1, keepdims=True)
        share_row = live_row * jnp.sum(jnp.where(is_mate_t, live_col, 0.0), axis=0, keepdims=True)
        coef_col = (share_col / total_col).astype(BF16).astype(F32)
        coef_row = (share_row / total_row).astype(BF16).astype(F32)
        mixing = expo * (coef_col * live_row + coef_row * live_col) - 2.0 * jnp.where(is_mate, share_col, 0.0)
        dunit = dot(mixing.astype(BF16), unit_b, 1, 0) * (LOSS_SCALE / TAU)
        along = jnp.sum(unit * dunit, axis=1, keepdims=True)
        dproj = ((dunit - unit * along) * inv).astype(BF16)
        dproj_ref[...] = dproj.astype(F32)
        mine = dproj_ref[pl.ds(pl.multiple_of(rank * 8, 8), 8), :].astype(BF16)
        dpooled = dot(mine, head, 1, 1).astype(BF16)
        top = (dpooled.astype(F32) / (ph * pw)).astype(BF16).astype(F32)
        for r in range(cap):
            cot_ref[r * ph * pw : (r + 1) * ph * pw, :] = jnp.broadcast_to(top[r : r + 1], (ph * pw, ch))

    def relay_copy():
        return pltpu.make_async_remote_copy(
            src_ref=out_ref, dst_ref=relay_ref,
            send_sem=cs_sem.at[0], recv_sem=cr_sem.at[0],
            device_id=(lax.rem(sec + S - 1, S), rank), device_id_type=MESH)

    def build_lhs():
        for off in range(1, D):
            x_copy(off).wait()
        lane = lax.broadcasted_iota(jnp.int32, (cp, rows), 1)
        w = lane % pw
        h = (lane // pw) % ph

        def one(d, carry):
            xd = xg_ref[d].astype(F32)
            for i in range(3):
                for j in range(3):
                    s = (i - 1) * pw + (j - 1)
                    v = xd if s == 0 else pltpu.roll(xd, (-s) % rows, 1)
                    ok = (h + (i - 1) >= 0) & (h + (i - 1) < ph) & (w + (j - 1) >= 0) & (w + (j - 1) < pw)
                    t = 3 * i + j
                    lhs_ref[d, t * cp : (t + 1) * cp, :] = jnp.where(ok, v, 0.0).astype(BF16)
            return carry

        lax.fori_loop(0, D, one, 0)

    @pl.when(sec != last)
    def _():
        build_lhs()
        relay_copy().wait_recv()
        cot_ref[...] = relay_ref[...].astype(F32)

    def d_copy(off):
        return pltpu.make_async_remote_copy(
            src_ref=dg_ref.at[rank], dst_ref=dg_ref.at[rank],
            send_sem=ds_sem.at[off - 1], recv_sem=dr_sem.at[off - 1],
            device_id=(sec, peer(off)), device_id_type=MESH)

    cot = cot_ref[...]
    dpre = (cot * slope_ref[...]).astype(BF16)
    dg_ref[rank] = dpre

    @pl.when(sec == 0)
    def _():
        for off in range(1, D):
            d_copy(off).start()

    fill_patches(patch_ref, dpre.astype(F32), (cap, ph, pw), True)
    below = cot_ref[...] + dot(patch_ref[...], kt_ref[...], 1, 0)
    out_ref[...] = below.astype(BF16)
    dx_ref[0] = below.reshape(cap, ph, pw, ch).astype(BF16)

    @pl.when(sec > 0)
    def _():
        relay_copy().start()
        for off in range(1, D):
            d_copy(off).start()

    @pl.when(sec == last)
    def _():
        build_lhs()
        n = D * 8
        g = g_ref[...].reshape(n, ch + 128)
        pt = g[:, :ch].T
        for p in range(D):
            pt_ref[p, 0:cw] = pt[p * cw : (p + 1) * cw]
        own = pt_ref[rank].astype(BF16)
        hg = dot(own, dproj_ref[...].astype(BF16), 1, 0)
        for s in range(S):
            hgs_ref[s] = hg[:, s * ew : (s + 1) * ew]
        for off in range(1, S):
            head_copy(off).start()

    acc_ref[...] = dot(lhs_ref[rank], dg_ref[rank], 1, 0)

    def gather_step(off, carry):
        d_copy(off).wait()
        d = source(off)
        acc_ref[...] += dot(lhs_ref[d], dg_ref[d], 1, 0)
        return carry

    lax.fori_loop(1, D, gather_step, 0)
    for t in range(9):
        wg_ref[t] = acc_ref[t * cp : t * cp + cw, :]

    @pl.when(sec == last)
    def _():
        hg_ref[...] = hgs_ref[last, 0:cw, :]
        for off in range(1, S):
            head_copy(off).wait_send()

    @pl.when(sec != last)
    def _():
        head_copy(1).wait_recv()
        hg_ref[...] = hgr_ref[0:cw, :]

    @pl.when(sec > 0)
    def _():
        relay_copy().wait_send()


def per_device(mesh_sizes, saved, kernels, head, counts, pairs, valid):
    S, D = mesh_sizes
    _, cap, ph, pw, ch = saved.shape
    emb = head.shape[1]
    cw = ch // D
    cp = -(-cw // 16) * 16
    rows = cap * ph * pw
    taps = jnp.transpose(kernels[0], (1, 2, 0, 3)).reshape(9, ch, ch)
    cfg = (S, D, cap, ph, pw, ch, emb, cw, cp)
    vmem = pl.BlockSpec(memory_space=pltpu.VMEM)
    smem = pl.BlockSpec(memory_space=pltpu.SMEM)
    sem = pltpu.SemaphoreType.DMA
    dx, wg, hg = pl.pallas_call(
        functools.partial(body, cfg),
        out_shape=(
            jax.ShapeDtypeStruct((1, cap, ph, pw, ch), BF16),
            jax.ShapeDtypeStruct((9, cw, ch), F32),
            jax.ShapeDtypeStruct((cw, emb // S), F32),
        ),
        in_specs=[vmem, pl.BlockSpec(memory_space=pl.ANY), vmem, smem, smem, smem],
        out_specs=(vmem, vmem, vmem),
        scratch_shapes=[
            pltpu.VMEM((9, ch, ch), BF16),
            pltpu.VMEM((9 * ch, ch), BF16),
            pltpu.VMEM((rows, 9 * ch), BF16),
            pltpu.VMEM((rows, ch), F32),
            pltpu.VMEM((8, ch + 128), F32),
            pltpu.VMEM((D, 8, ch + 128), F32),
            pltpu.VMEM((D * 8, emb), F32),
            pltpu.VMEM((D, cp, D * 8), F32),
            pltpu.VMEM((S, cp, emb // S), F32),
            pltpu.VMEM((cp, emb // S), F32),
            pltpu.VMEM((D, cp, rows), BF16),
            pltpu.VMEM((D, cp, rows), BF16),
            pltpu.VMEM((D, 9 * cp, rows), BF16),
            pltpu.VMEM((D, rows, ch), BF16),
            pltpu.VMEM((9 * cp, ch), F32),
            pltpu.VMEM((rows, ch), F32),
            pltpu.VMEM((rows, ch), BF16),
            pltpu.VMEM((rows, ch), BF16),
            sem((3,)),
            sem((D - 1,)), sem((D - 1,)),
            sem((S - 1,)), sem((1,)),
            sem((D - 1,)), sem((D - 1,)),
            sem((D - 1,)), sem((D - 1,)),
            sem((1,)), sem((1,)),
        ],
        compiler_params=pltpu.CompilerParams(
            collective_id=0, has_side_effects=True, vmem_limit_bytes=50 * 2**20
        ),
    )(saved, taps, head, counts, pairs, valid)
    wgrad = jnp.transpose(wg.reshape(3, 3, cw, ch), (2, 0, 1, 3))
    return dx, wgrad[None], hg


def solution(mesh):
    sizes = (mesh.shape["section"], mesh.shape["dp"])
    return jax.shard_map(
        functools.partial(per_device, sizes),
        mesh=mesh,
        in_specs=(
            P("section", "dp", None, None, None),
            P("section", None, None, None, None),
            P(),
            P("dp"),
            P("dp"),
            P("dp"),
        ),
        out_specs=(
            P("section", "dp", None, None, None),
            P("section", "dp", None, None, None),
            P("dp", "section"),
        ),
        check_vma=False,
    )
```

```python
import functools

import jax
import jax.numpy as jnp
from jax import lax
from jax.experimental import pallas as pl
from jax.experimental.pallas import tpu as pltpu
from jax.sharding import PartitionSpec as P

TAU = 0.2
LOSS_SCALE = 32.0
EPS = 1e-06
MESH = pl.DeviceIdType.MESH
F32 = jnp.float32
BF16 = jnp.bfloat16
HBM = pltpu.HBM


def dot(a, b, ca, cb):
    return lax.dot_general(a, b, (((ca,), (cb,)), ((), ())), preferred_element_type=F32)


def fill_patches(dst_ref, v, dims, flip):
    recs, ph, pw = dims
    rows, ch = v.shape
    w = lax.broadcasted_iota(jnp.int32, (rows, ch), 0) % pw
    for j in range(3):
        if j == 1:
            vj = v
        elif j == 0:
            vj = jnp.where(w > 0, pltpu.roll(v, 1, 0), 0.0)
        else:
            vj = jnp.where(w < pw - 1, pltpu.roll(v, rows - 1, 0), 0.0)
        cells = vj.reshape(recs, ph, pw, ch)
        edge = jnp.zeros((recs, 1, pw, ch), F32)
        for i in range(3):
            if i == 1:
                vij = cells
            elif i == 0:
                vij = jnp.concatenate([edge, cells[:, : ph - 1]], axis=1)
            else:
                vij = jnp.concatenate([cells[:, 1:], edge], axis=1)
            tap = 3 * i + j
            if flip:
                tap = 8 - tap
            dst_ref[:, tap * ch : (tap + 1) * ch] = vij.reshape(rows, ch).astype(BF16)


def body(cfg, x_hbm, k_hbm, head_hbm, counts_hbm, pairs_hbm, valid_hbm,
         dx_hbm, wg_hbm, hg_hbm, dx_ref, wg_ref, hg_ref, out_sem,
         x_ref, head_ref, counts_ref, pairs_ref, valid_ref,
         k_ref, kt0_ref, kt1_ref, patch_ref, patch0_ref, patch1_ref, part_ref, slope_ref,
         pooled_ref, g_ref, dproj_ref, pt_ref,
         hgs_ref, hgr_ref, xt_ref, xg_ref, lhs_ref, dg0_ref, dg1_ref, acc0_ref, acc1_ref,
         top_ref, relay0_ref, relay1_ref, out0_ref, out1_ref,
         in_sem, k_sem, gs_sem, gr_sem, hs_sem, hr_sem, xs_sem, xr_sem,
         ds_sem, dr_sem, fs_sem, fr_sem, cs_sem, cr_sem):
    S, D, cap, ph, pw, ch, emb, cw, cp, c0 = cfg
    C = D // 2
    rows = cap * ph * pw
    cells = ph * pw
    sec = lax.axis_index("section")
    rank = lax.axis_index("dp")
    chip = rank // 2
    core = rank % 2
    partner = chip * 2 + 1 - core
    last = S - 1
    span = ((0, c0), (c0, ch))
    dg = (dg0_ref, dg1_ref)
    acc = (acc0_ref, acc1_ref)
    relay = (relay0_ref, relay1_ref)
    out = (out0_ref, out1_ref)
    patches = (patch0_ref, patch1_ref)
    kt = (kt0_ref, kt1_ref)

    def peer(off):
        return lax.rem(rank + off, D)

    x_in = pltpu.make_async_copy(x_hbm, x_ref, in_sem.at[0])
    x_in.start()
    k_copies = []
    for i in range(3):
        cpy = pltpu.make_async_copy(k_hbm.at[3 * i : 3 * i + 3], k_ref.at[3 * i : 3 * i + 3], k_sem.at[i])
        cpy.start()
        k_copies.append(cpy)
    small = [
        pltpu.make_async_copy(counts_hbm, counts_ref, in_sem.at[1]),
        pltpu.make_async_copy(pairs_hbm, pairs_ref, in_sem.at[2]),
        pltpu.make_async_copy(valid_hbm, valid_ref, in_sem.at[3]),
        pltpu.make_async_copy(head_hbm, head_ref, in_sem.at[4]),
    ]
    for cpy in small:
        cpy.start()

    barrier = pltpu.get_barrier_semaphore()
    for off in range(1, D):
        pl.semaphore_signal(barrier, inc=1, device_id=(sec, peer(off)), device_id_type=MESH)
    for off in range(1, S):
        pl.semaphore_signal(barrier, inc=1, device_id=(lax.rem(sec + off, S), rank), device_id_type=MESH)

    x_in.wait()
    x = x_ref[0].astype(F32).reshape(rows, ch)
    fill_patches(patch_ref, x, (cap, ph, pw), False)
    pre = None
    for i in range(3):
        k_copies[i].wait()
        kk = k_ref[3 * i : 3 * i + 3].reshape(3 * ch, ch)
        term = dot(patch_ref[:, 3 * i * ch : 3 * (i + 1) * ch], kk, 1, 0)
        pre = term if pre is None else pre + term
    sig = 1.0 / (1.0 + jnp.exp(-pre))
    slope_ref[...] = sig * (1.0 + pre * (1.0 - sig))
    for cpy in small:
        cpy.wait()

    pl.semaphore_wait(barrier, D - 1 + S - 1)

    def pooled_copy(off):
        return pltpu.make_async_remote_copy(
            src_ref=g_ref.at[rank], dst_ref=g_ref.at[rank],
            send_sem=gs_sem.at[off - 1], recv_sem=gr_sem.at[off - 1],
            device_id=(sec, peer(off)), device_id_type=MESH)

    @pl.when(sec == last)
    def _():
        y = x + pre * sig
        mean = jnp.sum(y.reshape(cap, cells, ch), axis=1) * (1.0 / cells)
        mean = mean.astype(BF16).astype(F32)
        pooled_ref[...] = jnp.zeros(pooled_ref.shape, F32)
        pooled_ref[0:cap, :ch] = mean
        row = lax.broadcasted_iota(jnp.int32, (8, 128), 0)
        lane = lax.broadcasted_iota(jnp.int32, (8, 128), 1)
        meta = jnp.where(lane == 1, -1.0, 0.0)
        for r in range(cap):
            live = jnp.where((r < counts_ref[0]) & (valid_ref[r] == 1), 1.0, 0.0)
            p = pairs_ref[r]
            pid = ((p // cap) * 8 + p % cap).astype(F32)
            meta = jnp.where((row == r) & (lane == 0), live, meta)
            meta = jnp.where((row == r) & (lane == 1), pid, meta)
        pooled_ref[:, ch:] = meta
        g_ref[rank] = pooled_ref[...]
        for off in range(1, D):
            pooled_copy(off).start()

    def x_copy(off):
        return pltpu.make_async_remote_copy(
            src_ref=xt_ref.at[peer(off)], dst_ref=xg_ref.at[rank],
            send_sem=xs_sem.at[off - 1], recv_sem=xr_sem.at[off - 1],
            device_id=(sec, peer(off)), device_id_type=MESH)

    xt = x.T
    for p in range(D):
        blk = xt[p * cw : (p + 1) * cw]
        if cp != cw:
            blk = jnp.concatenate([blk, jnp.zeros((cp - cw, rows), F32)], axis=0)
        xt_ref[p] = blk.astype(BF16)
    xg_ref[rank] = xt_ref[rank]
    for off in range(1, D):
        x_copy(off).start()

    for t in range(9):
        kt_t = k_ref[t].T
        kt0_ref[t * c0 : (t + 1) * c0, :] = kt_t[:c0]
        kt1_ref[t * (ch - c0) : (t + 1) * (ch - c0), :] = kt_t[c0:]

    ew = emb // S

    def head_copy(off):
        to = lax.rem(sec + off, S)
        return pltpu.make_async_remote_copy(
            src_ref=hgs_ref.at[to], dst_ref=hgr_ref,
            send_sem=hs_sem.at[off - 1], recv_sem=hr_sem.at[0],
            device_id=(to, rank), device_id_type=MESH)

    @pl.when(sec == last)
    def _():
        for off in range(1, D):
            pooled_copy(off).wait()
        n = D * 8
        g = g_ref[...].reshape(n, ch + 128)
        pooled = g[:, :ch].astype(BF16)
        meta = g[:, ch:]
        meta_t = meta.T
        live_col, pair_col = meta[:, 0:1], meta[:, 1:2]
        live_row, pair_row = meta_t[0:1, :], meta_t[1:2, :]
        ii = lax.broadcasted_iota(jnp.int32, (n, n), 0)
        jj = lax.broadcasted_iota(jnp.int32, (n, n), 1)
        head = head_ref[...]
        proj = dot(pooled, head, 1, 0)
        inv = lax.rsqrt(jnp.sum(proj * proj, axis=1, keepdims=True) + EPS)
        unit = proj * inv
        unit_b = unit.astype(BF16)
        scores = dot(unit_b, unit_b, 1, 1) / TAU
        expo = jnp.where(ii != jj, jnp.exp(scores), 0.0)
        is_mate = pair_col == jj.astype(F32)
        is_mate_t = pair_row == ii.astype(F32)
        total_col = jnp.sum(expo * live_row, axis=1, keepdims=True)
        total_row = jnp.sum(expo * live_col, axis=0, keepdims=True)
        share_col = live_col * jnp.sum(jnp.where(is_mate, live_row, 0.0), axis=1, keepdims=True)
        share_row = live_row * jnp.sum(jnp.where(is_mate_t, live_col, 0.0), axis=0, keepdims=True)
        coef_col = (share_col / total_col).astype(BF16).astype(F32)
        coef_row = (share_row / total_row).astype(BF16).astype(F32)
        mixing = expo * (coef_col * live_row + coef_row * live_col) - 2.0 * jnp.where(is_mate, share_col, 0.0)
        dunit = dot(mixing.astype(BF16), unit_b, 1, 0) * (LOSS_SCALE / TAU)
        along = jnp.sum(unit * dunit, axis=1, keepdims=True)
        dproj = ((dunit - unit * along) * inv).astype(BF16)
        dproj_ref[...] = dproj.astype(F32)
        mine = dproj_ref[pl.ds(pl.multiple_of(rank * 8, 8), 8), :].astype(BF16)
        dpooled = dot(mine, head, 1, 1).astype(BF16)
        top = (dpooled.astype(F32) / cells).astype(BF16).astype(F32)
        for q, (lo, hi) in enumerate(span):
            for r in range(cap):
                relay[q][r * cells : (r + 1) * cells, :] = jnp.broadcast_to(
                    top[r : r + 1, lo:hi], (cells, hi - lo)).astype(BF16)

    def relay_copy(q):
        return pltpu.make_async_remote_copy(
            src_ref=out[q], dst_ref=relay[q],
            send_sem=cs_sem.at[q], recv_sem=cr_sem.at[q],
            device_id=(lax.rem(sec + S - 1, S), rank), device_id_type=MESH)

    def build_lhs():
        for off in range(1, D):
            x_copy(off).wait()
        lane = lax.broadcasted_iota(jnp.int32, (cp, rows), 1)
        w = lane % pw
        h = (lane // pw) % ph

        def one(d, carry):
            xd = xg_ref[d].astype(F32)
            for i in range(3):
                for j in range(3):
                    s = (i - 1) * pw + (j - 1)
                    v = xd if s == 0 else pltpu.roll(xd, (-s) % rows, 1)
                    ok = (h + (i - 1) >= 0) & (h + (i - 1) < ph) & (w + (j - 1) >= 0) & (w + (j - 1) < pw)
                    t = 3 * i + j
                    lhs_ref[d, t * cp : (t + 1) * cp, :] = jnp.where(ok, v, 0.0).astype(BF16)
            return carry

        lax.fori_loop(0, D, one, 0)

    @pl.when(sec != last)
    def _():
        build_lhs()

    def near_copy(q):
        return pltpu.make_async_remote_copy(
            src_ref=dg[q].at[rank], dst_ref=dg[q].at[rank],
            send_sem=ds_sem.at[q, 0], recv_sem=dr_sem.at[q, 0],
            device_id=(sec, partner), device_id_type=MESH)

    def far_copy(q, off):
        return pltpu.make_async_remote_copy(
            src_ref=dg[q].at[rank], dst_ref=dg[q].at[rank],
            send_sem=ds_sem.at[q, off], recv_sem=dr_sem.at[q, off],
            device_id=(sec, lax.rem(chip + off, C) * 2 + core), device_id_type=MESH)

    def far_source(off):
        return lax.rem(chip + C - off, C) * 2

    def forward(q, off):
        d = far_source(off) + core
        return pltpu.make_async_remote_copy(
            src_ref=dg[q].at[d], dst_ref=dg[q].at[d],
            send_sem=fs_sem.at[q, off - 1], recv_sem=fr_sem.at[q, off - 1],
            device_id=(sec, partner), device_id_type=MESH)

    def start_gather(q):
        for off in range(1, C):
            far_copy(q, off).start()
        near_copy(q).start()

    cots = []
    for q, (lo, hi) in enumerate(span):
        @pl.when(sec != last)
        def _():
            relay_copy(q).wait_recv()

        cot = relay[q][...].astype(F32)
        dpre = (cot * slope_ref[:, lo:hi]).astype(BF16)
        dg[q][rank] = dpre

        @pl.when(sec == 0)
        def _():
            start_gather(q)

        fill_patches(patches[q], dpre.astype(F32), (cap, ph, pw), True)
        if q == 0:
            part_ref[...] = dot(patches[0][...], kt[0][...], 1, 0)

    for q, (lo, hi) in enumerate(span):
        below = relay[q][...].astype(F32) + (
            part_ref[:, lo:hi] + dot(patches[1][...], kt[1][:, lo:hi], 1, 0))
        out[q][...] = below.astype(BF16)

        @pl.when(sec > 0)
        def _():
            relay_copy(q).start()

        dx_ref[0, :, :, :, lo:hi] = below.reshape(cap, ph, pw, hi - lo).astype(BF16)

    dx_out = pltpu.make_async_copy(dx_ref, dx_hbm, out_sem.at[0])
    dx_out.start()

    @pl.when(sec > 0)
    def _():
        for q in range(2):
            start_gather(q)

    @pl.when(sec == last)
    def _():
        build_lhs()
        n = D * 8
        g = g_ref[...].reshape(n, ch + 128)
        pt = g[:, :ch].T
        for p in range(D):
            pt_ref[p, 0:cw] = pt[p * cw : (p + 1) * cw]
        own = pt_ref[rank].astype(BF16)
        hg = dot(own, dproj_ref[...].astype(BF16), 1, 0)
        for s in range(S):
            hgs_ref[s] = hg[:, s * ew : (s + 1) * ew]
        for off in range(1, S):
            head_copy(off).start()

    def add_block(d, q):
        acc[q][...] += dot(lhs_ref[d], dg[q][d], 1, 0)

    for q in range(2):
        acc[q][...] = dot(lhs_ref[rank], dg[q][rank], 1, 0)

    def far_step(off, carry):
        for q in range(2):
            far_copy(q, off).wait()
            forward(q, off).start()
        for q in range(2):
            add_block(far_source(off) + core, q)
        return carry

    lax.fori_loop(1, C, far_step, 0)

    for q in range(2):
        near_copy(q).wait()
        add_block(partner, q)

    def forward_step(off, carry):
        for q in range(2):
            forward(q, off).wait()
            add_block(far_source(off) + 1 - core, q)
        return carry

    lax.fori_loop(1, C, forward_step, 0)
    wg_out = []
    for i in range(3):
        for t in range(3 * i, 3 * i + 3):
            for q, (lo, hi) in enumerate(span):
                wg_ref[t, :, lo:hi] = acc[q][t * cp : t * cp + cw, :]
        part_i = pl.ds(3 * i, 3)
        cpy = pltpu.make_async_copy(wg_ref.at[part_i], wg_hbm.at[part_i], out_sem.at[2 + i])
        cpy.start()
        wg_out.append(cpy)

    @pl.when(sec == last)
    def _():
        hg_ref[...] = hgs_ref[last, 0:cw, :]
        for off in range(1, S):
            head_copy(off).wait_send()

    @pl.when(sec != last)
    def _():
        head_copy(1).wait_recv()
        hg_ref[...] = hgr_ref[0:cw, :]

    hg_out = pltpu.make_async_copy(hg_ref, hg_hbm, out_sem.at[1])
    hg_out.start()
    for cpy in [dx_out, hg_out] + wg_out:
        cpy.wait()

    @pl.when(sec > 0)
    def _():
        for q in range(2):
            relay_copy(q).wait_send()


def leave(a_ref, b_ref, c_ref, ao_ref, bo_ref, co_ref, sems):
    copies = [
        pltpu.make_async_copy(b_ref.at[pl.ds(i, 1)], bo_ref.at[pl.ds(i, 1)], sems.at[2 + i])
        for i in range(9)
    ]
    copies.append(pltpu.make_async_copy(a_ref, ao_ref, sems.at[0]))
    copies.append(pltpu.make_async_copy(c_ref, co_ref, sems.at[1]))
    for cpy in copies:
        cpy.start()
    for cpy in copies:
        cpy.wait()


def per_device(mesh_sizes, saved, kernels, head, counts, pairs, valid):
    S, D = mesh_sizes
    _, cap, ph, pw, ch = saved.shape
    emb = head.shape[1]
    cw = ch // D
    cp = -(-cw // 16) * 16
    c0 = (ch - 1) // 256 * 256
    c1 = ch - c0
    rows = cap * ph * pw
    taps = jnp.transpose(kernels[0], (1, 2, 0, 3)).reshape(9, ch, ch)
    cfg = (S, D, cap, ph, pw, ch, emb, cw, cp, c0)
    hbm = pl.BlockSpec(memory_space=HBM)
    sem = pltpu.SemaphoreType.DMA
    shapes = (
        jax.ShapeDtypeStruct((1, cap, ph, pw, ch), BF16),
        jax.ShapeDtypeStruct((9, cw, ch), F32),
        jax.ShapeDtypeStruct((cw, emb // S), F32),
    )
    results = pl.pallas_call(
        functools.partial(body, cfg),
        out_shape=shapes,
        in_specs=[hbm] * 6,
        out_specs=(hbm,) * 3,
        scratch_shapes=[
            pltpu.VMEM(shapes[0].shape, BF16),
            pltpu.VMEM(shapes[1].shape, F32),
            pltpu.VMEM(shapes[2].shape, F32),
            sem((5,)),
            pltpu.VMEM(saved.shape, BF16),
            pltpu.VMEM(head.shape, BF16),
            pltpu.SMEM(counts.shape, jnp.int32),
            pltpu.SMEM(pairs.shape, jnp.int32),
            pltpu.SMEM(valid.shape, jnp.int32),
            pltpu.VMEM((9, ch, ch), BF16),
            pltpu.VMEM((9 * c0, ch), BF16),
            pltpu.VMEM((9 * c1, ch), BF16),
            pltpu.VMEM((rows, 9 * ch), BF16),
            pltpu.VMEM((rows, 9 * c0), BF16),
            pltpu.VMEM((rows, 9 * c1), BF16),
            pltpu.VMEM((rows, ch), F32),
            pltpu.VMEM((rows, ch), F32),
            pltpu.VMEM((8, ch + 128), F32),
            pltpu.VMEM((D, 8, ch + 128), F32),
            pltpu.VMEM((D * 8, emb), F32),
            pltpu.VMEM((D, cp, D * 8), F32),
            pltpu.VMEM((S, cp, emb // S), F32),
            pltpu.VMEM((cp, emb // S), F32),
            pltpu.VMEM((D, cp, rows), BF16),
            pltpu.VMEM((D, cp, rows), BF16),
            pltpu.VMEM((D, 9 * cp, rows), BF16),
            pltpu.VMEM((D, rows, c0), BF16),
            pltpu.VMEM((D, rows, c1), BF16),
            pltpu.VMEM((9 * cp, c0), F32),
            pltpu.VMEM((9 * cp, c1), F32),
            pltpu.VMEM((8, ch), F32),
            pltpu.VMEM((rows, c0), BF16),
            pltpu.VMEM((rows, c1), BF16),
            pltpu.VMEM((rows, c0), BF16),
            pltpu.VMEM((rows, c1), BF16),
            sem((5,)),
            sem((3,)),
            sem((D - 1,)), sem((D - 1,)),
            sem((S - 1,)), sem((1,)),
            sem((D - 1,)), sem((D - 1,)),
            sem((2, D // 2)), sem((2, D // 2)),
            sem((2, D // 2)), sem((2, D // 2)),
            sem((2,)), sem((2,)),
        ],
        compiler_params=pltpu.CompilerParams(
            collective_id=0, has_side_effects=True, vmem_limit_bytes=60 * 2**20
        ),
    )(saved, taps, head, counts, pairs, valid)
    dx, wg, hg = pl.pallas_call(
        leave,
        out_shape=shapes,
        in_specs=[hbm] * 3,
        out_specs=(hbm,) * 3,
        scratch_shapes=[sem((11,))],
        compiler_params=pltpu.CompilerParams(vmem_limit_bytes=60 * 2**20),
    )(*results)
    wgrad = jnp.transpose(wg.reshape(3, 3, cw, ch), (2, 0, 1, 3))
    return dx, wgrad[None], hg


def solution(mesh):
    sizes = (mesh.shape["section"], mesh.shape["dp"])
    return jax.shard_map(
        functools.partial(per_device, sizes),
        mesh=mesh,
        in_specs=(
            P("section", "dp", None, None, None),
            P("section", None, None, None, None),
            P(),
            P("dp"),
            P("dp"),
            P("dp"),
        ),
        out_specs=(
            P("section", "dp", None, None, None),
            P("section", "dp", None, None, None),
            P("dp", "section"),
        ),
        check_vma=False,
    )
```

```python
import functools

import jax
import jax.numpy as jnp
from jax import lax
from jax.experimental import pallas as pl
from jax.experimental.pallas import tpu as pltpu
from jax.sharding import PartitionSpec as P

TAU = 0.2
LOSS_SCALE = 32.0
EPS = 1e-06
MESH = pl.DeviceIdType.MESH
F32 = jnp.float32
BF16 = jnp.bfloat16
HBM = pltpu.HBM


def dot(a, b, ca, cb):
    return lax.dot_general(a, b, (((ca,), (cb,)), ((), ())), preferred_element_type=F32)


def fill_patches(dst_ref, v, dims, flip):
    recs, ph, pw = dims
    rows, ch = v.shape
    w = lax.broadcasted_iota(jnp.int32, (rows, ch), 0) % pw
    for j in range(3):
        if j == 1:
            vj = v
        elif j == 0:
            vj = jnp.where(w > 0, pltpu.roll(v, 1, 0), 0.0)
        else:
            vj = jnp.where(w < pw - 1, pltpu.roll(v, rows - 1, 0), 0.0)
        cells = vj.reshape(recs, ph, pw, ch)
        edge = jnp.zeros((recs, 1, pw, ch), F32)
        for i in range(3):
            if i == 1:
                vij = cells
            elif i == 0:
                vij = jnp.concatenate([edge, cells[:, : ph - 1]], axis=1)
            else:
                vij = jnp.concatenate([cells[:, 1:], edge], axis=1)
            tap = 3 * i + j
            if flip:
                tap = 8 - tap
            dst_ref[:, tap * ch : (tap + 1) * ch] = vij.reshape(rows, ch).astype(BF16)


def body(cfg, x_hbm, k_hbm, head_hbm, counts_hbm, pairs_hbm, valid_hbm,
         dx_ref, wg_ref, hg_ref,
         x_ref, head_ref, counts_ref, pairs_ref, valid_ref,
         k_ref, kt0_ref, kt1_ref, patch_ref, patch0_ref, patch1_ref, part_ref, slope_ref,
         pooled_ref, g_ref, dproj_ref, pt_ref,
         hgs_ref, hgr_ref, xt_ref, xg_ref, lhs_ref, dg0_ref, dg1_ref, acc0_ref, acc1_ref,
         top_ref, relay0_ref, relay1_ref, out0_ref, out1_ref,
         in_sem, k_sem, gs_sem, gr_sem, hs_sem, hr_sem, xs_sem, xr_sem,
         ds_sem, dr_sem, fs_sem, fr_sem, cs_sem, cr_sem):
    S, D, cap, ph, pw, ch, emb, cw, cp, c0 = cfg
    C = D // 2
    rows = cap * ph * pw
    cells = ph * pw
    sec = lax.axis_index("section")
    rank = lax.axis_index("dp")
    chip = rank // 2
    core = rank % 2
    partner = chip * 2 + 1 - core
    last = S - 1
    span = ((0, c0), (c0, ch))
    dg = (dg0_ref, dg1_ref)
    acc = (acc0_ref, acc1_ref)
    relay = (relay0_ref, relay1_ref)
    out = (out0_ref, out1_ref)
    patches = (patch0_ref, patch1_ref)
    kt = (kt0_ref, kt1_ref)

    def peer(off):
        return lax.rem(rank + off, D)

    x_in = pltpu.make_async_copy(x_hbm, x_ref, in_sem.at[0])
    x_in.start()
    k_copies = []
    for i in range(3):
        cpy = pltpu.make_async_copy(k_hbm.at[3 * i : 3 * i + 3], k_ref.at[3 * i : 3 * i + 3], k_sem.at[i])
        cpy.start()
        k_copies.append(cpy)
    small = [
        pltpu.make_async_copy(counts_hbm, counts_ref, in_sem.at[1]),
        pltpu.make_async_copy(pairs_hbm, pairs_ref, in_sem.at[2]),
        pltpu.make_async_copy(valid_hbm, valid_ref, in_sem.at[3]),
        pltpu.make_async_copy(head_hbm, head_ref, in_sem.at[4]),
    ]
    for cpy in small:
        cpy.start()

    barrier = pltpu.get_barrier_semaphore()
    for off in range(1, D):
        pl.semaphore_signal(barrier, inc=1, device_id=(sec, peer(off)), device_id_type=MESH)
    for off in range(1, S):
        pl.semaphore_signal(barrier, inc=1, device_id=(lax.rem(sec + off, S), rank), device_id_type=MESH)

    x_in.wait()
    x = x_ref[0].astype(F32).reshape(rows, ch)
    fill_patches(patch_ref, x, (cap, ph, pw), False)
    pre = None
    for i in range(3):
        k_copies[i].wait()
        kk = k_ref[3 * i : 3 * i + 3].reshape(3 * ch, ch)
        term = dot(patch_ref[:, 3 * i * ch : 3 * (i + 1) * ch], kk, 1, 0)
        pre = term if pre is None else pre + term
    sig = 1.0 / (1.0 + jnp.exp(-pre))
    slope_ref[...] = sig * (1.0 + pre * (1.0 - sig))
    for cpy in small:
        cpy.wait()

    pl.semaphore_wait(barrier, D - 1 + S - 1)

    def pooled_copy(off):
        return pltpu.make_async_remote_copy(
            src_ref=g_ref.at[rank], dst_ref=g_ref.at[rank],
            send_sem=gs_sem.at[off - 1], recv_sem=gr_sem.at[off - 1],
            device_id=(sec, peer(off)), device_id_type=MESH)

    @pl.when(sec == last)
    def _():
        y = x + pre * sig
        mean = jnp.sum(y.reshape(cap, cells, ch), axis=1) * (1.0 / cells)
        mean = mean.astype(BF16).astype(F32)
        pooled_ref[...] = jnp.zeros(pooled_ref.shape, F32)
        pooled_ref[0:cap, :ch] = mean
        row = lax.broadcasted_iota(jnp.int32, (8, 128), 0)
        lane = lax.broadcasted_iota(jnp.int32, (8, 128), 1)
        meta = jnp.where(lane == 1, -1.0, 0.0)
        for r in range(cap):
            live = jnp.where((r < counts_ref[0]) & (valid_ref[r] == 1), 1.0, 0.0)
            p = pairs_ref[r]
            pid = ((p // cap) * 8 + p % cap).astype(F32)
            meta = jnp.where((row == r) & (lane == 0), live, meta)
            meta = jnp.where((row == r) & (lane == 1), pid, meta)
        pooled_ref[:, ch:] = meta
        g_ref[rank] = pooled_ref[...]
        for off in range(1, D):
            pooled_copy(off).start()

    def x_copy(off):
        return pltpu.make_async_remote_copy(
            src_ref=xt_ref.at[peer(off)], dst_ref=xg_ref.at[rank],
            send_sem=xs_sem.at[off - 1], recv_sem=xr_sem.at[off - 1],
            device_id=(sec, peer(off)), device_id_type=MESH)

    def send_inputs():
        xt = x_ref[0].astype(F32).reshape(rows, ch).T
        for p in range(D):
            blk = xt[p * cw : (p + 1) * cw]
            if cp != cw:
                blk = jnp.concatenate([blk, jnp.zeros((cp - cw, rows), F32)], axis=0)
            xt_ref[p] = blk.astype(BF16)
        xg_ref[rank] = xt_ref[rank]
        for off in range(1, D):
            x_copy(off).start()

    @pl.when(sec != last)
    def _():
        send_inputs()

    for t in range(9):
        kt_t = k_ref[t].T
        kt0_ref[t * c0 : (t + 1) * c0, :] = kt_t[:c0]
        kt1_ref[t * (ch - c0) : (t + 1) * (ch - c0), :] = kt_t[c0:]

    ew = emb // S

    def head_copy(off):
        to = lax.rem(sec + off, S)
        return pltpu.make_async_remote_copy(
            src_ref=hgs_ref.at[to], dst_ref=hgr_ref,
            send_sem=hs_sem.at[off - 1], recv_sem=hr_sem.at[0],
            device_id=(to, rank), device_id_type=MESH)

    @pl.when(sec == last)
    def _():
        for off in range(1, D):
            pooled_copy(off).wait()
        n = D * 8
        g = g_ref[...].reshape(n, ch + 128)
        pooled = g[:, :ch].astype(BF16)
        meta = g[:, ch:]
        meta_t = meta.T
        live_col, pair_col = meta[:, 0:1], meta[:, 1:2]
        live_row, pair_row = meta_t[0:1, :], meta_t[1:2, :]
        ii = lax.broadcasted_iota(jnp.int32, (n, n), 0)
        jj = lax.broadcasted_iota(jnp.int32, (n, n), 1)
        head = head_ref[...]
        proj = dot(pooled, head, 1, 0)
        inv = lax.rsqrt(jnp.sum(proj * proj, axis=1, keepdims=True) + EPS)
        unit = proj * inv
        unit_b = unit.astype(BF16)
        scores = dot(unit_b, unit_b, 1, 1) / TAU
        expo = jnp.where(ii != jj, jnp.exp(scores), 0.0)
        is_mate = pair_col == jj.astype(F32)
        is_mate_t = pair_row == ii.astype(F32)
        total_col = jnp.sum(expo * live_row, axis=1, keepdims=True)
        total_row = jnp.sum(expo * live_col, axis=0, keepdims=True)
        share_col = live_col * jnp.sum(jnp.where(is_mate, live_row, 0.0), axis=1, keepdims=True)
        share_row = live_row * jnp.sum(jnp.where(is_mate_t, live_col, 0.0), axis=0, keepdims=True)
        coef_col = (share_col / total_col).astype(BF16).astype(F32)
        coef_row = (share_row / total_row).astype(BF16).astype(F32)
        mixing = expo * (coef_col * live_row + coef_row * live_col) - 2.0 * jnp.where(is_mate, share_col, 0.0)
        dunit = dot(mixing.astype(BF16), unit_b, 1, 0) * (LOSS_SCALE / TAU)
        along = jnp.sum(unit * dunit, axis=1, keepdims=True)
        dproj = ((dunit - unit * along) * inv).astype(BF16)
        dproj_ref[...] = dproj.astype(F32)
        mine = dproj_ref[pl.ds(pl.multiple_of(rank * 8, 8), 8), :].astype(BF16)
        dpooled = dot(mine, head, 1, 1).astype(BF16)
        top = (dpooled.astype(F32) / cells).astype(BF16).astype(F32)
        for q, (lo, hi) in enumerate(span):
            for r in range(cap):
                relay[q][r * cells : (r + 1) * cells, :] = jnp.broadcast_to(
                    top[r : r + 1, lo:hi], (cells, hi - lo)).astype(BF16)

    def relay_copy(q):
        return pltpu.make_async_remote_copy(
            src_ref=out[q], dst_ref=relay[q],
            send_sem=cs_sem.at[q], recv_sem=cr_sem.at[q],
            device_id=(lax.rem(sec + S - 1, S), rank), device_id_type=MESH)

    def build_lhs():
        for off in range(1, D):
            x_copy(off).wait()
        lane = lax.broadcasted_iota(jnp.int32, (cp, rows), 1)
        w = lane % pw
        h = (lane // pw) % ph

        def one(d, carry):
            xd = xg_ref[d].astype(F32)
            for i in range(3):
                for j in range(3):
                    s = (i - 1) * pw + (j - 1)
                    v = xd if s == 0 else pltpu.roll(xd, (-s) % rows, 1)
                    ok = (h + (i - 1) >= 0) & (h + (i - 1) < ph) & (w + (j - 1) >= 0) & (w + (j - 1) < pw)
                    t = 3 * i + j
                    lhs_ref[d, t * cp : (t + 1) * cp, :] = jnp.where(ok, v, 0.0).astype(BF16)
            return carry

        lax.fori_loop(0, D, one, 0)

    @pl.when(sec != last)
    def _():
        build_lhs()

    def near_copy(q):
        return pltpu.make_async_remote_copy(
            src_ref=dg[q].at[rank], dst_ref=dg[q].at[rank],
            send_sem=ds_sem.at[q, 0], recv_sem=dr_sem.at[q, 0],
            device_id=(sec, partner), device_id_type=MESH)

    def far_copy(q, off):
        return pltpu.make_async_remote_copy(
            src_ref=dg[q].at[rank], dst_ref=dg[q].at[rank],
            send_sem=ds_sem.at[q, off], recv_sem=dr_sem.at[q, off],
            device_id=(sec, lax.rem(chip + off, C) * 2 + core), device_id_type=MESH)

    def far_source(off):
        return lax.rem(chip + C - off, C) * 2

    def forward(q, off):
        d = far_source(off) + core
        return pltpu.make_async_remote_copy(
            src_ref=dg[q].at[d], dst_ref=dg[q].at[d],
            send_sem=fs_sem.at[q, off - 1], recv_sem=fr_sem.at[q, off - 1],
            device_id=(sec, partner), device_id_type=MESH)

    def start_gather(q):
        for off in range(1, C):
            far_copy(q, off).start()
        near_copy(q).start()

    cots = []
    for q, (lo, hi) in enumerate(span):
        @pl.when(sec != last)
        def _():
            relay_copy(q).wait_recv()

        cot = relay[q][...].astype(F32)
        dpre = (cot * slope_ref[:, lo:hi]).astype(BF16)
        dg[q][rank] = dpre

        @pl.when(sec == 0)
        def _():
            start_gather(q)

        fill_patches(patches[q], dpre.astype(F32), (cap, ph, pw), True)
        if q == 0:
            part_ref[...] = dot(patches[0][...], kt[0][...], 1, 0)

    for q, (lo, hi) in enumerate(span):
        below = relay[q][...].astype(F32) + (
            part_ref[:, lo:hi] + dot(patches[1][...], kt[1][:, lo:hi], 1, 0))
        out[q][...] = below.astype(BF16)

        @pl.when(sec > 0)
        def _():
            relay_copy(q).start()

        dx_ref[0, :, :, :, lo:hi] = below.reshape(cap, ph, pw, hi - lo).astype(BF16)

    @pl.when(sec > 0)
    def _():
        for q in range(2):
            start_gather(q)

        @pl.when(sec == last)
        def _():
            send_inputs()

    @pl.when(sec == last)
    def _():
        build_lhs()
        n = D * 8
        g = g_ref[...].reshape(n, ch + 128)
        pt = g[:, :ch].T
        for p in range(D):
            pt_ref[p, 0:cw] = pt[p * cw : (p + 1) * cw]
        own = pt_ref[rank].astype(BF16)
        hg = dot(own, dproj_ref[...].astype(BF16), 1, 0)
        for s in range(S):
            hgs_ref[s] = hg[:, s * ew : (s + 1) * ew]
        for off in range(1, S):
            head_copy(off).start()

    def add_block(d, q):
        acc[q][...] += dot(lhs_ref[d], dg[q][d], 1, 0)

    for q in range(2):
        acc[q][...] = dot(lhs_ref[rank], dg[q][rank], 1, 0)

    def far_step(off, carry):
        for q in range(2):
            far_copy(q, off).wait()
            forward(q, off).start()
        for q in range(2):
            add_block(far_source(off) + core, q)
        return carry

    lax.fori_loop(1, C, far_step, 0)

    for q in range(2):
        near_copy(q).wait()
        add_block(partner, q)

    def forward_step(off, carry):
        for q in range(2):
            forward(q, off).wait()
            add_block(far_source(off) + 1 - core, q)
        return carry

    lax.fori_loop(1, C, forward_step, 0)
    for q, (lo, hi) in enumerate(span):
        for t in range(9):
            wg_ref[t, :, lo:hi] = acc[q][t * cp : t * cp + cw, :]

    @pl.when(sec == last)
    def _():
        hg_ref[...] = hgs_ref[last, 0:cw, :]
        for off in range(1, S):
            head_copy(off).wait_send()

    @pl.when(sec != last)
    def _():
        head_copy(1).wait_recv()
        hg_ref[...] = hgr_ref[0:cw, :]

    @pl.when(sec > 0)
    def _():
        for q in range(2):
            relay_copy(q).wait_send()


def leave(a_ref, b_ref, c_ref, ao_ref, bo_ref, co_ref, sems):
    copies = [
        pltpu.make_async_copy(b_ref.at[pl.ds(i, 1)], bo_ref.at[pl.ds(i, 1)], sems.at[2 + i])
        for i in range(9)
    ]
    copies.append(pltpu.make_async_copy(a_ref, ao_ref, sems.at[0]))
    copies.append(pltpu.make_async_copy(c_ref, co_ref, sems.at[1]))
    for cpy in copies:
        cpy.start()
    for cpy in copies:
        cpy.wait()


def per_device(mesh_sizes, saved, kernels, head, counts, pairs, valid):
    S, D = mesh_sizes
    _, cap, ph, pw, ch = saved.shape
    emb = head.shape[1]
    cw = ch // D
    cp = -(-cw // 16) * 16
    c0 = (ch - 1) // 256 * 256
    c1 = ch - c0
    rows = cap * ph * pw
    taps = jnp.transpose(kernels[0], (1, 2, 0, 3)).reshape(9, ch, ch)
    cfg = (S, D, cap, ph, pw, ch, emb, cw, cp, c0)
    hbm = pl.BlockSpec(memory_space=HBM)
    vmem = pl.BlockSpec(memory_space=pltpu.VMEM)
    sem = pltpu.SemaphoreType.DMA
    shapes = (
        jax.ShapeDtypeStruct((1, cap, ph, pw, ch), BF16),
        jax.ShapeDtypeStruct((9, cw, ch), F32),
        jax.ShapeDtypeStruct((cw, emb // S), F32),
    )
    results = pl.pallas_call(
        functools.partial(body, cfg),
        out_shape=tuple(pltpu.VMEM(v.shape, v.dtype) for v in shapes),
        in_specs=[hbm] * 6,
        out_specs=(vmem,) * 3,
        scratch_shapes=[
            pltpu.VMEM(saved.shape, BF16),
            pltpu.VMEM(head.shape, BF16),
            pltpu.SMEM(counts.shape, jnp.int32),
            pltpu.SMEM(pairs.shape, jnp.int32),
            pltpu.SMEM(valid.shape, jnp.int32),
            pltpu.VMEM((9, ch, ch), BF16),
            pltpu.VMEM((9 * c0, ch), BF16),
            pltpu.VMEM((9 * c1, ch), BF16),
            pltpu.VMEM((rows, 9 * ch), BF16),
            pltpu.VMEM((rows, 9 * c0), BF16),
            pltpu.VMEM((rows, 9 * c1), BF16),
            pltpu.VMEM((rows, ch), F32),
            pltpu.VMEM((rows, ch), F32),
            pltpu.VMEM((8, ch + 128), F32),
            pltpu.VMEM((D, 8, ch + 128), F32),
            pltpu.VMEM((D * 8, emb), F32),
            pltpu.VMEM((D, cp, D * 8), F32),
            pltpu.VMEM((S, cp, emb // S), F32),
            pltpu.VMEM((cp, emb // S), F32),
            pltpu.VMEM((D, cp, rows), BF16),
            pltpu.VMEM((D, cp, rows), BF16),
            pltpu.VMEM((D, 9 * cp, rows), BF16),
            pltpu.VMEM((D, rows, c0), BF16),
            pltpu.VMEM((D, rows, c1), BF16),
            pltpu.VMEM((9 * cp, c0), F32),
            pltpu.VMEM((9 * cp, c1), F32),
            pltpu.VMEM((8, ch), F32),
            pltpu.VMEM((rows, c0), BF16),
            pltpu.VMEM((rows, c1), BF16),
            pltpu.VMEM((rows, c0), BF16),
            pltpu.VMEM((rows, c1), BF16),
            sem((5,)),
            sem((3,)),
            sem((D - 1,)), sem((D - 1,)),
            sem((S - 1,)), sem((1,)),
            sem((D - 1,)), sem((D - 1,)),
            sem((2, D // 2)), sem((2, D // 2)),
            sem((2, D // 2)), sem((2, D // 2)),
            sem((2,)), sem((2,)),
        ],
        compiler_params=pltpu.CompilerParams(
            collective_id=0, has_side_effects=True, vmem_limit_bytes=58 * 2**20
        ),
    )(saved, taps, head, counts, pairs, valid)
    dx, wg, hg = pl.pallas_call(
        leave,
        out_shape=shapes,
        in_specs=[vmem] * 3,
        out_specs=(hbm,) * 3,
        scratch_shapes=[sem((11,))],
        compiler_params=pltpu.CompilerParams(vmem_limit_bytes=4 * 2**20),
    )(*results)
    wgrad = jnp.transpose(wg.reshape(3, 3, cw, ch), (2, 0, 1, 3))
    return dx, wgrad[None], hg


def solution(mesh):
    sizes = (mesh.shape["section"], mesh.shape["dp"])
    return jax.shard_map(
        functools.partial(per_device, sizes),
        mesh=mesh,
        in_specs=(
            P("section", "dp", None, None, None),
            P("section", None, None, None, None),
            P(),
            P("dp"),
            P("dp"),
            P("dp"),
        ),
        out_specs=(
            P("section", "dp", None, None, None),
            P("section", "dp", None, None, None),
            P("dp", "section"),
        ),
        check_vma=False,
    )
```

```python
import functools

import jax
import jax.numpy as jnp
from jax import lax
from jax.experimental import pallas as pl
from jax.experimental.pallas import tpu as pltpu
from jax.sharding import PartitionSpec as P

TAU = 0.2
LOSS_SCALE = 32.0
EPS = 1e-06
MESH = pl.DeviceIdType.MESH
F32 = jnp.float32
BF16 = jnp.bfloat16
HBM = pltpu.HBM


def dot(a, b, ca, cb):
    return lax.dot_general(a, b, (((ca,), (cb,)), ((), ())), preferred_element_type=F32)


def fill_patches(dst_ref, v, dims, flip):
    recs, ph, pw = dims
    rows, ch = v.shape
    w = lax.broadcasted_iota(jnp.int32, (rows, ch), 0) % pw
    for j in range(3):
        if j == 1:
            vj = v
        elif j == 0:
            vj = jnp.where(w > 0, pltpu.roll(v, 1, 0), 0.0)
        else:
            vj = jnp.where(w < pw - 1, pltpu.roll(v, rows - 1, 0), 0.0)
        cells = vj.reshape(recs, ph, pw, ch)
        edge = jnp.zeros((recs, 1, pw, ch), F32)
        for i in range(3):
            if i == 1:
                vij = cells
            elif i == 0:
                vij = jnp.concatenate([edge, cells[:, : ph - 1]], axis=1)
            else:
                vij = jnp.concatenate([cells[:, 1:], edge], axis=1)
            tap = 3 * i + j
            if flip:
                tap = 8 - tap
            dst_ref[:, tap * ch : (tap + 1) * ch] = vij.reshape(rows, ch).astype(BF16)


def body(cfg, x_hbm, k_hbm, head_hbm, counts_hbm, pairs_hbm, valid_hbm,
         dx_ref, wg_ref, hg_ref,
         x_ref, head_ref, counts_ref, pairs_ref, valid_ref,
         k_ref, kt0_ref, kt1_ref, patch_ref, patch0_ref, patch1_ref, part_ref, slope_ref,
         pooled_ref, g_ref, dproj_ref, pt_ref,
         hgs_ref, hgr_ref, xt_ref, xg_ref, lhs_ref, dg0_ref, dg1_ref, acc0_ref, acc1_ref,
         top_ref, relay0_ref, relay1_ref, out0_ref, out1_ref,
         in_sem, k_sem, gs_sem, gr_sem, hs_sem, hr_sem, xs_sem, xr_sem,
         ds_sem, dr_sem, fs_sem, fr_sem, cs_sem, cr_sem):
    S, D, cap, ph, pw, ch, emb, cw, cp, c0 = cfg
    C = D // 2
    rows = cap * ph * pw
    cells = ph * pw
    sec = lax.axis_index("section")
    rank = lax.axis_index("dp")
    chip = rank // 2
    core = rank % 2
    partner = chip * 2 + 1 - core
    last = S - 1
    span = ((0, c0), (c0, ch))
    dg = (dg0_ref, dg1_ref)
    acc = (acc0_ref, acc1_ref)
    relay = (relay0_ref, relay1_ref)
    out = (out0_ref, out1_ref)
    patches = (patch0_ref, patch1_ref)
    kt = (kt0_ref, kt1_ref)

    def peer(off):
        return lax.rem(rank + off, D)

    x_in = pltpu.make_async_copy(x_hbm, x_ref, in_sem.at[0])
    x_in.start()
    k_copies = []
    for i in range(3):
        cpy = pltpu.make_async_copy(k_hbm.at[3 * i : 3 * i + 3], k_ref.at[3 * i : 3 * i + 3], k_sem.at[i])
        cpy.start()
        k_copies.append(cpy)
    small = [
        pltpu.make_async_copy(counts_hbm, counts_ref, in_sem.at[1]),
        pltpu.make_async_copy(pairs_hbm, pairs_ref, in_sem.at[2]),
        pltpu.make_async_copy(valid_hbm, valid_ref, in_sem.at[3]),
        pltpu.make_async_copy(head_hbm, head_ref, in_sem.at[4]),
    ]
    for cpy in small:
        cpy.start()

    barrier = pltpu.get_barrier_semaphore()
    for off in range(1, D):
        pl.semaphore_signal(barrier, inc=1, device_id=(sec, peer(off)), device_id_type=MESH)
    for off in range(1, S):
        pl.semaphore_signal(barrier, inc=1, device_id=(lax.rem(sec + off, S), rank), device_id_type=MESH)

    x_in.wait()
    x = x_ref[0].astype(F32).reshape(rows, ch)
    fill_patches(patch_ref, x, (cap, ph, pw), False)
    pre = None
    for i in range(3):
        k_copies[i].wait()
        kk = k_ref[3 * i : 3 * i + 3].reshape(3 * ch, ch)
        term = dot(patch_ref[:, 3 * i * ch : 3 * (i + 1) * ch], kk, 1, 0)
        pre = term if pre is None else pre + term
    sig = 1.0 / (1.0 + jnp.exp(-pre))
    slope_ref[...] = sig * (1.0 + pre * (1.0 - sig))
    for cpy in small:
        cpy.wait()

    pl.semaphore_wait(barrier, D - 1 + S - 1)

    def pooled_copy(off):
        return pltpu.make_async_remote_copy(
            src_ref=g_ref.at[rank], dst_ref=g_ref.at[rank],
            send_sem=gs_sem.at[off - 1], recv_sem=gr_sem.at[off - 1],
            device_id=(sec, peer(off)), device_id_type=MESH)

    @pl.when(sec == last)
    def _():
        y = x + pre * sig
        mean = jnp.sum(y.reshape(cap, cells, ch), axis=1) * (1.0 / cells)
        mean = mean.astype(BF16).astype(F32)
        pooled_ref[...] = jnp.zeros(pooled_ref.shape, F32)
        pooled_ref[0:cap, :ch] = mean
        row = lax.broadcasted_iota(jnp.int32, (8, 128), 0)
        lane = lax.broadcasted_iota(jnp.int32, (8, 128), 1)
        meta = jnp.where(lane == 1, -1.0, 0.0)
        for r in range(cap):
            live = jnp.where((r < counts_ref[0]) & (valid_ref[r] == 1), 1.0, 0.0)
            p = pairs_ref[r]
            pid = ((p // cap) * 8 + p % cap).astype(F32)
            meta = jnp.where((row == r) & (lane == 0), live, meta)
            meta = jnp.where((row == r) & (lane == 1), pid, meta)
        pooled_ref[:, ch:] = meta
        g_ref[rank] = pooled_ref[...]
        for off in range(1, D):
            pooled_copy(off).start()

    def x_copy(off):
        return pltpu.make_async_remote_copy(
            src_ref=xt_ref.at[peer(off)], dst_ref=xg_ref.at[rank],
            send_sem=xs_sem.at[off - 1], recv_sem=xr_sem.at[off - 1],
            device_id=(sec, peer(off)), device_id_type=MESH)

    def send_inputs():
        xt = x_ref[0].astype(F32).reshape(rows, ch).T
        for p in range(D):
            blk = xt[p * cw : (p + 1) * cw]
            if cp != cw:
                blk = jnp.concatenate([blk, jnp.zeros((cp - cw, rows), F32)], axis=0)
            xt_ref[p] = blk.astype(BF16)
        xg_ref[rank] = xt_ref[rank]
        for off in range(1, D):
            x_copy(off).start()

    @pl.when(sec != last)
    def _():
        send_inputs()

    for t in range(9):
        kt_t = k_ref[t].T
        kt0_ref[t * c0 : (t + 1) * c0, :] = kt_t[:c0]
        kt1_ref[t * (ch - c0) : (t + 1) * (ch - c0), :] = kt_t[c0:]

    ew = emb // S

    def head_copy(off):
        to = lax.rem(sec + off, S)
        return pltpu.make_async_remote_copy(
            src_ref=hgs_ref.at[to], dst_ref=hgr_ref,
            send_sem=hs_sem.at[off - 1], recv_sem=hr_sem.at[0],
            device_id=(to, rank), device_id_type=MESH)

    @pl.when(sec == last)
    def _():
        for off in range(1, D):
            pooled_copy(off).wait()
        n = D * 8
        g = g_ref[...].reshape(n, ch + 128)
        pooled = g[:, :ch].astype(BF16)
        meta = g[:, ch:]
        meta_t = meta.T
        live_col, pair_col = meta[:, 0:1], meta[:, 1:2]
        live_row, pair_row = meta_t[0:1, :], meta_t[1:2, :]
        ii = lax.broadcasted_iota(jnp.int32, (n, n), 0)
        jj = lax.broadcasted_iota(jnp.int32, (n, n), 1)
        head = head_ref[...]
        proj = dot(pooled, head, 1, 0)
        inv = lax.rsqrt(jnp.sum(proj * proj, axis=1, keepdims=True) + EPS)
        unit = proj * inv
        unit_b = unit.astype(BF16)
        scores = dot(unit_b, unit_b, 1, 1) / TAU
        expo = jnp.where(ii != jj, jnp.exp(scores), 0.0)
        is_mate = pair_col == jj.astype(F32)
        is_mate_t = pair_row == ii.astype(F32)
        total_col = jnp.sum(expo * live_row, axis=1, keepdims=True)
        total_row = jnp.sum(expo * live_col, axis=0, keepdims=True)
        share_col = live_col * jnp.sum(jnp.where(is_mate, live_row, 0.0), axis=1, keepdims=True)
        share_row = live_row * jnp.sum(jnp.where(is_mate_t, live_col, 0.0), axis=0, keepdims=True)
        coef_col = (share_col / total_col).astype(BF16).astype(F32)
        coef_row = (share_row / total_row).astype(BF16).astype(F32)
        mixing = expo * (coef_col * live_row + coef_row * live_col) - 2.0 * jnp.where(is_mate, share_col, 0.0)
        dunit = dot(mixing.astype(BF16), unit_b, 1, 0) * (LOSS_SCALE / TAU)
        along = jnp.sum(unit * dunit, axis=1, keepdims=True)
        dproj = ((dunit - unit * along) * inv).astype(BF16)
        dproj_ref[...] = dproj.astype(F32)
        mine = dproj_ref[pl.ds(pl.multiple_of(rank * 8, 8), 8), :].astype(BF16)
        dpooled = dot(mine, head, 1, 1).astype(BF16)
        top = (dpooled.astype(F32) / cells).astype(BF16).astype(F32)
        for q, (lo, hi) in enumerate(span):
            for r in range(cap):
                relay[q][r * cells : (r + 1) * cells, :] = jnp.broadcast_to(
                    top[r : r + 1, lo:hi], (cells, hi - lo)).astype(BF16)

    def relay_copy(q):
        return pltpu.make_async_remote_copy(
            src_ref=out[q], dst_ref=relay[q],
            send_sem=cs_sem.at[q], recv_sem=cr_sem.at[q],
            device_id=(lax.rem(sec + S - 1, S), rank), device_id_type=MESH)

    def build_lhs():
        for off in range(1, D):
            x_copy(off).wait()
        lane = lax.broadcasted_iota(jnp.int32, (cp, rows), 1)
        w = lane % pw
        h = (lane // pw) % ph

        def one(d, carry):
            xd = xg_ref[d].astype(F32)
            for i in range(3):
                for j in range(3):
                    s = (i - 1) * pw + (j - 1)
                    v = xd if s == 0 else pltpu.roll(xd, (-s) % rows, 1)
                    ok = (h + (i - 1) >= 0) & (h + (i - 1) < ph) & (w + (j - 1) >= 0) & (w + (j - 1) < pw)
                    t = 3 * i + j
                    lhs_ref[d, t * cp : (t + 1) * cp, :] = jnp.where(ok, v, 0.0).astype(BF16)
            return carry

        lax.fori_loop(0, D, one, 0)

    @pl.when(sec != last)
    def _():
        build_lhs()

    def near_copy(q):
        return pltpu.make_async_remote_copy(
            src_ref=dg[q].at[rank], dst_ref=dg[q].at[rank],
            send_sem=ds_sem.at[q, 0], recv_sem=dr_sem.at[q, 0],
            device_id=(sec, partner), device_id_type=MESH)

    def far_copy(q, off):
        return pltpu.make_async_remote_copy(
            src_ref=dg[q].at[rank], dst_ref=dg[q].at[rank],
            send_sem=ds_sem.at[q, off], recv_sem=dr_sem.at[q, off],
            device_id=(sec, lax.rem(chip + off, C) * 2 + core), device_id_type=MESH)

    def far_source(off):
        return lax.rem(chip + C - off, C) * 2

    def forward(q, off):
        d = far_source(off) + core
        return pltpu.make_async_remote_copy(
            src_ref=dg[q].at[d], dst_ref=dg[q].at[d],
            send_sem=fs_sem.at[q, off - 1], recv_sem=fr_sem.at[q, off - 1],
            device_id=(sec, partner), device_id_type=MESH)

    def start_gather(q):
        for off in range(1, C):
            far_copy(q, off).start()
        near_copy(q).start()

    cots = []
    for q, (lo, hi) in enumerate(span):
        @pl.when(sec != last)
        def _():
            relay_copy(q).wait_recv()

        cot = relay[q][...].astype(F32)
        dpre = (cot * slope_ref[:, lo:hi]).astype(BF16)
        dg[q][rank] = dpre

        @pl.when(sec == 0)
        def _():
            start_gather(q)

        fill_patches(patches[q], dpre.astype(F32), (cap, ph, pw), True)
        if q == 0:
            part_ref[...] = dot(patches[0][...], kt[0][...], 1, 0)

    for q, (lo, hi) in enumerate(span):
        below = relay[q][...].astype(F32) + (
            part_ref[:, lo:hi] + dot(patches[1][...], kt[1][:, lo:hi], 1, 0))
        out[q][...] = below.astype(BF16)

        @pl.when(sec > 0)
        def _():
            relay_copy(q).start()

        dx_ref[0, :, :, :, lo:hi] = below.reshape(cap, ph, pw, hi - lo).astype(BF16)

    @pl.when(sec > 0)
    def _():
        for q in range(2):
            start_gather(q)

        @pl.when(sec == last)
        def _():
            send_inputs()

    @pl.when(sec == last)
    def _():
        build_lhs()
        n = D * 8
        g = g_ref[...].reshape(n, ch + 128)
        pt = g[:, :ch].T
        for p in range(D):
            pt_ref[p, 0:cw] = pt[p * cw : (p + 1) * cw]
        own = pt_ref[rank].astype(BF16)
        hg = dot(own, dproj_ref[...].astype(BF16), 1, 0)
        for s in range(S):
            hgs_ref[s] = hg[:, s * ew : (s + 1) * ew]
        for off in range(1, S):
            head_copy(off).start()

    def add_block(d, q):
        acc[q][...] += dot(lhs_ref[d], dg[q][d], 1, 0)

    for q in range(2):
        acc[q][...] = dot(lhs_ref[rank], dg[q][rank], 1, 0)

    for q in range(2):
        near_copy(q).wait()
        add_block(partner, q)

    def far_step(off, carry):
        for q in range(2):
            far_copy(q, off).wait_recv()
            forward(q, off).start()
        return carry

    lax.fori_loop(1, C, far_step, 0)

    def far_add(off, carry):
        for q in range(2):
            add_block(far_source(off) + core, q)
        return carry

    lax.fori_loop(1, C, far_add, 0)

    def forward_step(off, carry):
        for q in range(2):
            far_copy(q, off).wait_send()
            forward(q, off).wait()
            add_block(far_source(off) + 1 - core, q)
        return carry

    lax.fori_loop(1, C, forward_step, 0)
    for q, (lo, hi) in enumerate(span):
        for t in range(9):
            wg_ref[t, :, lo:hi] = acc[q][t * cp : t * cp + cw, :]

    @pl.when(sec == last)
    def _():
        hg_ref[...] = hgs_ref[last, 0:cw, :]
        for off in range(1, S):
            head_copy(off).wait_send()

    @pl.when(sec != last)
    def _():
        head_copy(1).wait_recv()
        hg_ref[...] = hgr_ref[0:cw, :]

    @pl.when(sec > 0)
    def _():
        for q in range(2):
            relay_copy(q).wait_send()


def leave(a_ref, b_ref, c_ref, ao_ref, bo_ref, co_ref, sems):
    copies = [
        pltpu.make_async_copy(b_ref.at[pl.ds(i, 1)], bo_ref.at[pl.ds(i, 1)], sems.at[2 + i])
        for i in range(9)
    ]
    copies.append(pltpu.make_async_copy(a_ref, ao_ref, sems.at[0]))
    copies.append(pltpu.make_async_copy(c_ref, co_ref, sems.at[1]))
    for cpy in copies:
        cpy.start()
    for cpy in copies:
        cpy.wait()


def per_device(mesh_sizes, saved, kernels, head, counts, pairs, valid):
    S, D = mesh_sizes
    _, cap, ph, pw, ch = saved.shape
    emb = head.shape[1]
    cw = ch // D
    cp = -(-cw // 16) * 16
    c0 = (ch - 1) // 256 * 256
    c1 = ch - c0
    rows = cap * ph * pw
    taps = jnp.transpose(kernels[0], (1, 2, 0, 3)).reshape(9, ch, ch)
    cfg = (S, D, cap, ph, pw, ch, emb, cw, cp, c0)
    hbm = pl.BlockSpec(memory_space=HBM)
    vmem = pl.BlockSpec(memory_space=pltpu.VMEM)
    sem = pltpu.SemaphoreType.DMA
    shapes = (
        jax.ShapeDtypeStruct((1, cap, ph, pw, ch), BF16),
        jax.ShapeDtypeStruct((9, cw, ch), F32),
        jax.ShapeDtypeStruct((cw, emb // S), F32),
    )
    results = pl.pallas_call(
        functools.partial(body, cfg),
        out_shape=tuple(pltpu.VMEM(v.shape, v.dtype) for v in shapes),
        in_specs=[hbm] * 6,
        out_specs=(vmem,) * 3,
        scratch_shapes=[
            pltpu.VMEM(saved.shape, BF16),
            pltpu.VMEM(head.shape, BF16),
            pltpu.SMEM(counts.shape, jnp.int32),
            pltpu.SMEM(pairs.shape, jnp.int32),
            pltpu.SMEM(valid.shape, jnp.int32),
            pltpu.VMEM((9, ch, ch), BF16),
            pltpu.VMEM((9 * c0, ch), BF16),
            pltpu.VMEM((9 * c1, ch), BF16),
            pltpu.VMEM((rows, 9 * ch), BF16),
            pltpu.VMEM((rows, 9 * c0), BF16),
            pltpu.VMEM((rows, 9 * c1), BF16),
            pltpu.VMEM((rows, ch), F32),
            pltpu.VMEM((rows, ch), F32),
            pltpu.VMEM((8, ch + 128), F32),
            pltpu.VMEM((D, 8, ch + 128), F32),
            pltpu.VMEM((D * 8, emb), F32),
            pltpu.VMEM((D, cp, D * 8), F32),
            pltpu.VMEM((S, cp, emb // S), F32),
            pltpu.VMEM((cp, emb // S), F32),
            pltpu.VMEM((D, cp, rows), BF16),
            pltpu.VMEM((D, cp, rows), BF16),
            pltpu.VMEM((D, 9 * cp, rows), BF16),
            pltpu.VMEM((D, rows, c0), BF16),
            pltpu.VMEM((D, rows, c1), BF16),
            pltpu.VMEM((9 * cp, c0), F32),
            pltpu.VMEM((9 * cp, c1), F32),
            pltpu.VMEM((8, ch), F32),
            pltpu.VMEM((rows, c0), BF16),
            pltpu.VMEM((rows, c1), BF16),
            pltpu.VMEM((rows, c0), BF16),
            pltpu.VMEM((rows, c1), BF16),
            sem((5,)),
            sem((3,)),
            sem((D - 1,)), sem((D - 1,)),
            sem((S - 1,)), sem((1,)),
            sem((D - 1,)), sem((D - 1,)),
            sem((2, D // 2)), sem((2, D // 2)),
            sem((2, D // 2)), sem((2, D // 2)),
            sem((2,)), sem((2,)),
        ],
        compiler_params=pltpu.CompilerParams(
            collective_id=0, has_side_effects=True, vmem_limit_bytes=58 * 2**20
        ),
    )(saved, taps, head, counts, pairs, valid)
    dx, wg, hg = pl.pallas_call(
        leave,
        out_shape=shapes,
        in_specs=[vmem] * 3,
        out_specs=(hbm,) * 3,
        scratch_shapes=[sem((11,))],
        compiler_params=pltpu.CompilerParams(vmem_limit_bytes=4 * 2**20),
    )(*results)
    wgrad = jnp.transpose(wg.reshape(3, 3, cw, ch), (2, 0, 1, 3))
    return dx, wgrad[None], hg


def solution(mesh):
    sizes = (mesh.shape["section"], mesh.shape["dp"])
    return jax.shard_map(
        functools.partial(per_device, sizes),
        mesh=mesh,
        in_specs=(
            P("section", "dp", None, None, None),
            P("section", None, None, None, None),
            P(),
            P("dp"),
            P("dp"),
            P("dp"),
        ),
        out_specs=(
            P("section", "dp", None, None, None),
            P("section", "dp", None, None, None),
            P("dp", "section"),
        ),
        check_vma=False,
    )
```
